32 devices in a mesh: groups: 2 (over y), ctx: 16 (over z, x, core).
Axes of the slice: x: 2, y: 2, z: 4, core: 2. Of those that a mesh axis runs over, the one named last changes fastest.
Arguments:
- old_cache: bfloat16 [4096, 2048], P(('groups', 'ctx')), parts along dimension 0, may hold values from -10 to 10
- new_slot: int32 [4096], P(('groups', 'ctx')), parts along dimension 0, may hold values from -1 to 1023, as said below
- lengths: int32 [8], P('groups'), parts along dimension 0, may hold values from 1 to 768, 1024 in all
- old_angle: float32 [768, 64], replicated, may hold values from -3.15 to 3.15
- new_angle: float32 [768, 64], replicated, may hold values from -3.15 to 4.15
- queries: bfloat16 [64, 8192], P(('groups', 'ctx')), parts along dimension 0, may hold values from -128 to 128
- new_kv: bfloat16 [64, 2048], P(('groups', 'ctx')), parts along dimension 0, may hold values from -6 to 6
- resid: bfloat16 [64, 8192], P(('groups', 'ctx')), parts along dimension 0, may hold values from -6 to 6
- gain: bfloat16 [8192], replicated, may hold values from 0.25 to 1.75
- w_gate: bfloat16 [8192, 28672], P(None, 'ctx'), may hold values from -0.0625 to 0.0625
- w_up: bfloat16 [8192, 28672], P(None, 'ctx'), may hold values from -0.0625 to 0.0625
- w_down: bfloat16 [28672, 8192], P('ctx'), may hold values from -0.03125 to 0.03125
Outputs:
- new_cache: bfloat16 [2048, 2048], P(('groups', 'ctx')), parts along dimension 0
- layer_out: bfloat16 [64, 8192], P(('groups', 'ctx')), parts along dimension 0
The draws below stay inside these ranges and needn't reach their ends.
There are 2 independent parts, one for each index of `groups`. The reference program is written for one: setup_inputs(seed, part) draws one part's arguments, and reference() takes and returns one part's arrays. A program takes and returns all parts, laid end to end along the dimension named above; an argument that names none is the same for every part. Nothing has to cross between parts.
Inputs may be any that keep to these rules, and one draw needn't show every extreme that they name: `new_slot`: for slots below 1024: distinct slots of the new layout; the tokens of each holding device go to every device of ctx, exactly 8 to each. Slots from 1024 on hold -1.
All inputs are finite; a program needn't handle non-finite values.
Results may differ from the reference program's by a relative error of at most 0.0057.
Values may be sent and summed in bfloat16 or wider, within the bound.
A program may use at most 128 MiB of HBM per device.

```python
import math
import jax
import jax.numpy as jnp
import numpy as np
from jax import lax

D = 8192
QH = 64
KVH = 8
HD = 128
FF = 28672
CTOK_DEV = 64
SAMPLES = 4
SLOTS = 128
CACHE = 1024
R = 4
MAXLEN = 768
M = 32
G = 8
W = 2048
HALF = 64
N_CTX = 16


def draw_new_slot(key, part):
    per_peer = SLOTS // N_CTX
    first_key = jax.random.fold_in(key, 11)
    second_key = jax.random.fold_in(key, 23)
    sender_perm = jax.vmap(lambda sender: jax.random.permutation(jax.random.fold_in(first_key, sender), SLOTS))(jnp.arange(N_CTX, dtype=jnp.int32)).astype(jnp.int32)
    place_perm = jax.vmap(lambda target: jax.random.permutation(jax.random.fold_in(second_key, target), CTOK_DEV))(jnp.arange(N_CTX, dtype=jnp.int32)).astype(jnp.int32)
    slot_index = jnp.arange(N_CTX * SLOTS, dtype=jnp.int32)
    sender = slot_index // SLOTS
    local = slot_index % SLOTS
    mixed = sender_perm[sender, local]
    target = mixed // per_peer
    within = sender * per_peer + mixed % per_peer
    within = jnp.minimum(within, CTOK_DEV - 1)
    placed = target * CTOK_DEV + place_perm[target, within]
    return jnp.where(slot_index < CACHE, placed, -1).astype(jnp.int32)


def angle_tables(key):
    old_table = jax.random.uniform(jax.random.fold_in(key, 31), (MAXLEN, HALF), jnp.float32, -math.pi, math.pi)
    rates = jnp.exp(jax.random.uniform(jax.random.fold_in(key, 37), (HALF,), jnp.float32, math.log(0.03), math.log(1.0)))
    ramp = jnp.arange(MAXLEN, dtype=jnp.float32)[:, None] / float(MAXLEN)
    return (old_table, old_table + rates[None, :] * ramp)


def draw_old_angle(key, part):
    return angle_tables(key)[0]


def draw_new_angle(key, part):
    return angle_tables(key)[1]


def directions(key):
    base = jax.random.fold_in(key, 101)
    key_dir = jax.random.normal(jax.random.fold_in(base, 1), (KVH, HD), jnp.float32)
    sign_dir = jax.random.normal(jax.random.fold_in(base, 2), (KVH, HD), jnp.float32)
    value_dir = jnp.where(jax.random.uniform(jax.random.fold_in(base, 3), (KVH, HD), jnp.float32) < 0.5, -1.0, 1.0)
    return (key_dir, sign_dir, value_dir)


def draw_old_cache(key, part):
    total_rows = N_CTX * SLOTS
    key_dir, sign_dir, value_dir = directions(key)
    root = float(HD) ** 0.5
    signs = jnp.where(jax.random.uniform(jax.random.fold_in(key, 41), (total_rows, KVH), jnp.float32) < 0.5, -1.0, 1.0)
    blocks = total_rows // 256
    offset = jax.random.randint(jax.random.fold_in(key, 43), (blocks,), 0, 255)
    slot_index = jnp.arange(total_rows, dtype=jnp.int32)
    block_of = jnp.minimum(slot_index // 256, blocks - 1)
    within = slot_index % 256
    start_mark = within == offset[block_of]
    follow_mark = within == offset[block_of] + 1
    lift = jax.random.uniform(jax.random.fold_in(key, 47), (blocks,), jnp.float32, 1.5, 2.5)[block_of]
    shrink = jax.random.uniform(jax.random.fold_in(key, 53), (blocks,), jnp.float32, 0.004, 0.012)[block_of]
    key_noise = jnp.clip(jax.random.normal(jax.random.fold_in(key, 59), (total_rows, KVH, HD), jnp.float32), -6.0, 6.0)
    value_noise = jnp.clip(jax.random.normal(jax.random.fold_in(key, 61), (total_rows, KVH, HD), jnp.float32), -6.0, 6.0)
    level = 1.5 * jnp.where(start_mark | follow_mark, 1.0 + lift, 1.0)
    keys = 0.15 * key_noise + level[:, None, None] * key_dir[None] / root + signs[:, :, None] * sign_dir[None] / root
    keys = jnp.where(follow_mark[:, None, None], (1.0 - shrink)[:, None, None] * jnp.roll(keys, 1, axis=0), keys)
    values = 2.0 * signs[:, :, None] * value_dir[None] + 0.7 * value_noise
    joined = jnp.stack([keys, values], axis=1).reshape(total_rows, 2 * KVH * HD)
    return jnp.clip(joined, -10.0, 10.0).astype(jnp.bfloat16)


def draw_queries(key, part):
    key_dir, sign_dir, value_dir = directions(key)
    head_keys = jnp.repeat(key_dir, G, axis=0)
    head_signs_dir = jnp.repeat(sign_dir, G, axis=0)
    strength = jnp.exp(jax.random.uniform(jax.random.fold_in(key, 61), (M, 1), jnp.float32, math.log(0.8), math.log(3.5)))
    spread = jnp.exp(jax.random.uniform(jax.random.fold_in(key, 67), (M, QH), jnp.float32, math.log(0.85), math.log(1.18)))
    head_sign = jnp.where(jax.random.uniform(jax.random.fold_in(key, 71), (M, QH), jnp.float32) < 0.5, -1.0, 1.0)
    noise = 0.5 * jnp.clip(jax.random.normal(jax.random.fold_in(key, 5), (M, QH, HD), jnp.float32), -6.0, 6.0)
    base = (strength * spread)[:, :, None] * head_keys[None] + head_sign[:, :, None] * head_signs_dir[None] + noise
    return jnp.clip(base, -128.0, 128.0).reshape(M, D).astype(jnp.bfloat16)


def levels(stream_key, dims, shards, low, high):
    level = 1.0
    for axis_at, blocks in shards:
        heights = jax.random.uniform(jax.random.fold_in(jax.random.fold_in(stream_key, 6), axis_at), (blocks,), jnp.float32, low / len(shards), high / len(shards))
        level = level * jnp.repeat(jnp.exp(heights), dims[axis_at] // blocks).reshape((-1,) + (1,) * (len(dims) - 1 - axis_at))
    return level


def split_up(amount, total, reach, skew):
    weights = [(1 << 20) // math.isqrt(rank ** skew) + 1 for rank in range(2, amount + 1)]
    surplus, holding = total - reach - (amount - 1), [1] * (amount - 1)
    while surplus > 0:
        free = [i for i in range(amount - 1) if holding[i] < reach]
        pool, budget = sum([weights[i] for i in free]), surplus
        for i in free:
            addition = min(reach - holding[i], max(1, budget * weights[i] // pool), surplus)
            holding[i] = holding[i] + addition
            surplus = surplus - addition
    return np.array([reach] + holding)


def uneven(rng, number_of, total, limit, slope):
    if number_of == 2:
        one = jax.random.randint(rng, (), max(1, total - limit), min(limit, total - 1) + 1)
        return jnp.stack([one, total - one])
    sizes = jnp.asarray(split_up(number_of, total, limit, slope), jnp.int32)
    pairs = (number_of - 1) // 2
    giver, taker = sizes[1:1 + 2 * pairs:2], sizes[2:2 + 2 * pairs:2]
    margin = jnp.minimum(giver - 1, limit - taker)
    shifted = jax.random.randint(jax.random.fold_in(rng, 1), (pairs,), 0, 1 << 20) % (margin + 1)
    sizes = sizes.at[1:1 + 2 * pairs:2].set(giver - shifted).at[2:2 + 2 * pairs:2].set(taker + shifted)
    return sizes[jax.random.permutation(jax.random.fold_in(rng, 2), number_of)]


def normal_values(rng, dims, deviation, reach, pieces=(), held_as=jnp.bfloat16):
    values = jax.random.normal(rng, dims, jnp.float32) * deviation
    if len(pieces) > 0:
        values = levels(rng, dims, pieces, -0.22, 0.18) * values
    return jnp.clip(values, min=-reach, max=reach).astype(held_as)


def setup_inputs(seed: int = 0, part: int = 0) -> dict:
    arg_keys = jax.random.split(jax.random.key(seed), 13)
    own_keys = jax.random.split(jax.random.fold_in(arg_keys[12], part), 13)
    old_cache = draw_old_cache(jax.random.fold_in(jax.random.fold_in(arg_keys[12], part), 71), part)
    new_slot = draw_new_slot(jax.random.fold_in(jax.random.fold_in(arg_keys[12], part), 71), part)
    lengths = uneven(own_keys[2], R, CACHE, MAXLEN, 2).astype(jnp.int32)
    old_angle = draw_old_angle(jax.random.fold_in(arg_keys[12], 71), part)
    new_angle = draw_new_angle(jax.random.fold_in(arg_keys[12], 71), part)
    queries = draw_queries(jax.random.fold_in(jax.random.fold_in(arg_keys[12], part), 71), part)
    new_kv = normal_values(own_keys[6], (M, W), 1.0, 6.0, ((0, 16),))
    resid = normal_values(own_keys[7], (M, D), 1.0, 6.0, ((0, 16),))
    gain = jnp.clip(1.0 + 0.15 * jax.random.normal(arg_keys[8], (D,), jnp.float32), 0.25, 1.75).astype(jnp.bfloat16)
    w_gate = normal_values(arg_keys[9], (D, FF), D ** -0.5, 0.0625, ((1, 16),))
    w_up = normal_values(arg_keys[10], (D, FF), D ** -0.5, 0.0625, ((1, 16),))
    w_down = normal_values(arg_keys[11], (FF, D), FF ** -0.5, 0.03125, ((0, 16),))
    return dict(old_cache=old_cache, new_slot=new_slot, lengths=lengths, old_angle=old_angle, new_angle=new_angle, queries=queries, new_kv=new_kv, resid=resid, gain=gain, w_gate=w_gate, w_up=w_up, w_down=w_down)


def rotate_keys(block, where_pos, old_angle, new_angle):
    rows_here = block.shape[0]
    parts = block.reshape(rows_here, 2, KVH, HD)
    keys = parts[:, 0].astype(jnp.float32)
    delta = jnp.take(new_angle, where_pos, axis=0) - jnp.take(old_angle, where_pos, axis=0)
    cosine = jnp.cos(delta)[:, None, :]
    sine = jnp.sin(delta)[:, None, :]
    first = keys[..., :HALF]
    second = keys[..., HALF:]
    turned = jnp.concatenate([first * cosine - second * sine, second * cosine + first * sine], axis=-1).astype(jnp.bfloat16)
    return jnp.stack([turned, parts[:, 1]], axis=1).reshape(rows_here, 2 * KVH * HD)

def reference(old_cache, new_slot, lengths, old_angle, new_angle, queries, new_kv, resid, gain, w_gate, w_up, w_down):
    tokens = jnp.arange(CACHE, dtype=jnp.int32)
    row_ends = jnp.cumsum(lengths).astype(jnp.int32)
    token_row = jnp.searchsorted(row_ends, tokens, side='right').astype(jnp.int32)
    row_starts = (row_ends - lengths).astype(jnp.int32)
    token_pos = (tokens - jnp.take(row_starts, token_row)).astype(jnp.int32)
    turned = rotate_keys(old_cache[:CACHE], token_pos, old_angle, new_angle)
    new_cache = jnp.zeros((CACHE, 2 * KVH * HD), jnp.bfloat16).at[new_slot[:CACHE]].set(turned)
    cached = turned.reshape(CACHE, 2, KVH, HD)
    query_four = queries.reshape(M, KVH, G, HD)
    fresh_kv = new_kv.reshape(M // 2, 2, 2, KVH, HD)
    query_row = jnp.arange(M, dtype=jnp.int32) // (2 * SAMPLES)
    query_sample = jnp.arange(M, dtype=jnp.int32) // 2
    query_step = jnp.arange(M, dtype=jnp.int32) % 2
    matching = query_row[:, None] == token_row[None, :]
    own_steps = jnp.arange(2, dtype=jnp.int32)[None, :] <= query_step[:, None]
    fresh_rows = jnp.take(fresh_kv, query_sample, axis=0)
    scale = 1.0 / float(HD) ** 0.5
    high = lax.Precision.HIGHEST

    def one_head(head_index):
        query_head = jnp.take(query_four, head_index, axis=1).astype(jnp.float32)
        key_head = jnp.take(cached[:, 0], head_index, axis=1).astype(jnp.float32)
        value_head = jnp.take(cached[:, 1], head_index, axis=1).astype(jnp.float32)
        fresh_keys = jnp.take(fresh_rows[:, :, 0], head_index, axis=2).astype(jnp.float32)
        fresh_values = jnp.take(fresh_rows[:, :, 1], head_index, axis=2).astype(jnp.float32)
        scores = jnp.einsum('mge,ce->mgc', query_head, key_head, precision=high) * scale
        scores = jnp.where(matching[:, None, :], scores, -1e+30)
        own_scores = jnp.einsum('mge,mse->mgs', query_head, fresh_keys, precision=high) * scale
        own_scores = jnp.where(own_steps[:, None, :], own_scores, -1e+30)
        row_top = jnp.maximum(lax.optimization_barrier(jnp.max(scores, axis=-1)), lax.optimization_barrier(jnp.max(own_scores, axis=-1)))
        weights_cache = jnp.exp(scores - row_top[..., None])
        weights_own = jnp.exp(own_scores - row_top[..., None])
        summed = jnp.einsum('mgc,ce->mge', weights_cache, value_head, precision=high)
        summed = summed + jnp.einsum('mgs,mse->mge', weights_own, fresh_values, precision=high)
        totals = lax.optimization_barrier(jnp.sum(weights_cache, axis=-1)) + lax.optimization_barrier(jnp.sum(weights_own, axis=-1))
        return summed / totals[..., None]
    per_head = lax.map(one_head, jnp.arange(KVH, dtype=jnp.int32))
    attn = jnp.transpose(per_head, (1, 0, 2, 3)).reshape(M, QH * HD)
    hstate = resid.astype(jnp.float32) + attn
    normed = (hstate * lax.rsqrt(lax.optimization_barrier(jnp.mean(hstate * hstate, axis=-1, keepdims=True)) + 1e-05) * gain.astype(jnp.float32)).astype(jnp.bfloat16)
    gate_out = jnp.dot(normed, w_gate, preferred_element_type=jnp.float32)
    up_out = jnp.dot(normed, w_up, preferred_element_type=jnp.float32)
    hidden = (jax.nn.silu(gate_out) * up_out).astype(jnp.bfloat16)
    ffn_out = jnp.dot(hidden, w_down, preferred_element_type=jnp.float32)
    layer_out = (hstate + ffn_out).astype(jnp.bfloat16)
    return (new_cache, layer_out)
```

```python
import jax
import jax.numpy as jnp
from jax import lax
from jax.sharding import PartitionSpec as P

QH = 64
KVH = 8
HD = 128
CTOK_DEV = 64
SAMPLES = 4


def rotate_block(block, where_pos, old_angle, new_angle):
    rows_here = block.shape[0]
    half_size = HD // 2
    parts = block.reshape(rows_here, 2, KVH, HD)
    keys = parts[:, 0].astype(jnp.float32)
    delta = jnp.take(new_angle, where_pos, axis=0) - jnp.take(old_angle, where_pos, axis=0)
    cosine = jnp.cos(delta)[:, None, :]
    sine = jnp.sin(delta)[:, None, :]
    first = keys[..., :half_size]
    second = keys[..., half_size:]
    turned = jnp.concatenate(
        [first * cosine - second * sine, second * cosine + first * sine], axis=-1
    ).astype(jnp.bfloat16)
    return jnp.stack([turned, parts[:, 1]], axis=1).reshape(rows_here, 2 * KVH * HD)


def per_device(
    old_cache,
    new_slot,
    lengths,
    old_angle,
    new_angle,
    queries,
    new_kv,
    resid,
    gain,
    w_gate,
    w_up,
    w_down,
):
    devices = lax.axis_size("ctx")
    own_index = lax.axis_index("ctx")
    slot_count = old_cache.shape[0]
    row_width = old_cache.shape[1]
    per_peer = slot_count // devices
    rows_dev = queries.shape[0]
    all_rows = rows_dev * devices
    group_size = QH // KVH
    high = lax.Precision.HIGHEST
    scale = 1.0 / float(HD) ** 0.5
    tokens = own_index * slot_count + jnp.arange(slot_count, dtype=jnp.int32)
    requests = jnp.arange(lengths.shape[0], dtype=jnp.int32)
    row_ends = jnp.sum(jnp.where(requests[None, :] <= requests[:, None], lengths[None, :], 0), axis=1)
    passed = row_ends[None, :] <= tokens[:, None]
    owner_row = jnp.minimum(jnp.sum(passed.astype(jnp.int32), axis=1), lengths.shape[0] - 1)
    row_prior = jnp.sum(jnp.where(passed, lengths[None, :], 0), axis=1)
    position = jnp.clip(tokens - row_prior, 0, old_angle.shape[0] - 1)
    filled = new_slot >= 0
    all_queries = lax.all_gather(queries, "ctx", axis=0, tiled=True)
    target = jnp.where(
        filled, new_slot // CTOK_DEV, jnp.arange(slot_count, dtype=jnp.int32) // per_peer
    )
    sorted_order = jnp.argsort(target, stable=True)
    new_place = jnp.where(filled, new_slot % CTOK_DEV, -1)
    slot_info = jnp.stack([new_place, owner_row, position], axis=1)[sorted_order]
    sent_rows = old_cache[sorted_order].reshape(devices, per_peer, row_width)
    got_rows = lax.all_to_all(sent_rows, "ctx", split_axis=0, concat_axis=0, tiled=True)
    got_info = lax.all_to_all(
        slot_info.reshape(devices, per_peer, 3), "ctx", split_axis=0, concat_axis=0, tiled=True
    )
    got_rows = got_rows.reshape(slot_count, row_width)
    got_info = got_info.reshape(slot_count, 3)
    landing = jnp.where(got_info[:, 0] >= 0, got_info[:, 0], CTOK_DEV)
    placed = jnp.zeros((CTOK_DEV, row_width), jnp.bfloat16).at[landing].set(got_rows, mode="drop")
    placed_row = jnp.zeros((CTOK_DEV,), jnp.int32).at[landing].set(got_info[:, 1], mode="drop")
    placed_pos = jnp.zeros((CTOK_DEV,), jnp.int32).at[landing].set(got_info[:, 2], mode="drop")
    placed, moved_row, moved_pos = (placed, placed_row, placed_pos)
    new_cache = rotate_block(placed, moved_pos, old_angle, new_angle)
    key_count = new_cache.shape[0]
    key_split = new_cache.reshape(key_count, 2, KVH, HD)
    value_four = key_split[:, 1].astype(jnp.float32)
    query_four = all_queries.reshape(all_rows, KVH, group_size, HD)
    scores = (
        jnp.einsum(
            "mjge,cje->mjgc", query_four, key_split[:, 0], preferred_element_type=jnp.float32
        )
        * scale
    )
    query_row = jnp.arange(all_rows, dtype=jnp.int32) // (2 * SAMPLES)
    matching = query_row[:, None] == moved_row[None, :]
    scores = jnp.where(matching[:, None, None, :], scores, -1e30)
    local_top = jnp.max(scores, axis=-1)
    own_query = queries.reshape(rows_dev, KVH, group_size, HD).astype(jnp.float32)
    fresh_kv = jnp.repeat(new_kv.reshape(rows_dev // 2, 2, 2, KVH, HD), 2, axis=0).astype(
        jnp.float32
    )
    own_steps = (
        jnp.arange(2, dtype=jnp.int32)[None, :]
        <= (jnp.arange(rows_dev, dtype=jnp.int32) % 2)[:, None]
    )
    own_scores = jnp.einsum("mjge,msje->mjgs", own_query, fresh_kv[:, :, 0], precision=high) * scale
    own_scores = jnp.where(own_steps[:, None, None, :], own_scores, -1e30)
    own_top = jnp.max(own_scores, axis=-1)
    floor_top = jnp.maximum(local_top, -10000.0)
    weights_local = jnp.exp(scores - floor_top[..., None])
    summed = jnp.einsum("mjgc,cje->mjge", weights_local, value_four, precision=high)
    totals = jnp.sum(weights_local, axis=-1)
    got_sums, got_totals, got_tops = (
        lax.all_to_all(
            summed.reshape(devices, rows_dev, QH * HD),
            "ctx",
            split_axis=0,
            concat_axis=0,
            tiled=True,
        ),
        lax.all_to_all(
            totals.reshape(devices, rows_dev, QH), "ctx", split_axis=0, concat_axis=0, tiled=True
        ),
        lax.all_to_all(
            floor_top.reshape(devices, rows_dev, QH), "ctx", split_axis=0, concat_axis=0, tiled=True
        ),
    )
    got_tops = got_tops.reshape(devices, rows_dev, KVH, group_size)
    row_top = jnp.maximum(jnp.max(got_tops, axis=0), own_top)
    rescale = jnp.exp(got_tops - row_top[None])
    weights_own = jnp.exp(own_scores - row_top[..., None])
    row_sums = jnp.sum(
        rescale[..., None] * got_sums.reshape(devices, rows_dev, KVH, group_size, HD), axis=0
    )
    row_sums = row_sums + jnp.einsum(
        "mjgs,msje->mjge", weights_own, fresh_kv[:, :, 1], precision=high
    )
    row_totals = jnp.sum(
        rescale * got_totals.reshape(devices, rows_dev, KVH, group_size), axis=0
    ) + jnp.sum(weights_own, axis=-1)
    attn = (row_sums / row_totals[..., None]).reshape(rows_dev, QH * HD)
    hstate = resid.astype(jnp.float32) + attn
    normed = (
        hstate
        * lax.rsqrt(jnp.mean(hstate * hstate, axis=-1, keepdims=True) + 1e-05)
        * gain.astype(jnp.float32)
    ).astype(jnp.bfloat16)
    piece = lax.all_gather(normed, "ctx", axis=0, tiled=True)
    gate_out = jnp.dot(piece, w_gate, preferred_element_type=jnp.float32)
    up_out = jnp.dot(piece, w_up, preferred_element_type=jnp.float32)
    hidden_all = (jax.nn.silu(gate_out) * up_out).astype(jnp.bfloat16)
    ffn_out = lax.psum_scatter(
        jnp.dot(hidden_all, w_down, preferred_element_type=jnp.float32),
        "ctx",
        scatter_dimension=0,
        tiled=True,
    )
    layer_out = (hstate + ffn_out).astype(jnp.bfloat16)
    return (new_cache, layer_out)


def solution(mesh):
    return jax.shard_map(
        per_device,
        mesh=mesh,
        in_specs=(
            P(("groups", "ctx"), None),
            P(("groups", "ctx")),
            P("groups"),
            P(),
            P(),
            P(("groups", "ctx"), None),
            P(("groups", "ctx"), None),
            P(("groups", "ctx"), None),
            P(),
            P(None, "ctx"),
            P(None, "ctx"),
            P("ctx", None),
        ),
        out_specs=(P(("groups", "ctx"), None), P(("groups", "ctx"), None)),
        check_vma=False,
    )
```

```python
import jax
import jax.numpy as jnp
from jax import lax
from jax.experimental import pallas as pl
from jax.experimental.pallas import tpu as pltpu
from jax.sharding import PartitionSpec as P

QH = 64
KVH = 8
HD = 128
CTOK_DEV = 64
SAMPLES = 4

N = 16
HOLD = 8
PEER = 8
GROUP = QH // KVH
ROWS = 16
KC = 512
NG = 10
DC = 1024
ND = 3
MESH = pl.DeviceIdType.MESH


def remote(src, dst, send_sem, recv_sem, dev):
    return pltpu.make_async_remote_copy(
        src_ref=src,
        dst_ref=dst,
        send_sem=send_sem,
        recv_sem=recv_sem,
        device_id={"ctx": dev},
        device_id_type=MESH,
    )


def dot(a, b, dims=((1,), (0,))):
    return lax.dot_general(a, b, (dims, ((), ())), preferred_element_type=jnp.float32)


def split_dot(a, b):
    hi = a.astype(jnp.bfloat16)
    lo = (a - hi.astype(jnp.float32)).astype(jnp.bfloat16)
    return dot(hi, b) + dot(lo, b)


def kernel(
    old_cache, slots, lengths, old_angle, new_angle, pack, resid, gain,
    w_gate, w_up, w_down,
    new_cache, out,
    wg, wu, wd, kv, kvr, packr, sent, got, attn, attnr, norm, wide, xs, accg, accu,
    hidden, obuf, sbuf, rbuf, hst,
    g_sem, u_sem, d_sem, kv_s, kv_r, p_s, p_r, a_s, a_r, n_s, n_r, t_s, t_r, f_s, f_r,
):
    f32, bf16 = jnp.float32, jnp.bfloat16
    me = lax.axis_index("ctx")
    steps = w_gate.shape[0] // KC
    dsteps = w_down.shape[1] // DC
    holds = me < HOLD

    def fetch_in(c, s):
        rows = pl.ds(pl.multiple_of(c * KC, KC), KC)
        return (
            pltpu.make_async_copy(w_gate.at[rows, :], wg.at[s], g_sem.at[s]),
            pltpu.make_async_copy(w_up.at[rows, :], wu.at[s], u_sem.at[s]),
        )

    def fetch_out(c, s):
        cols = pl.ds(pl.multiple_of(c * DC, DC), DC)
        return pltpu.make_async_copy(w_down.at[:, cols], wd.at[s], d_sem.at[s])

    barrier = pltpu.get_barrier_semaphore()

    @pl.loop(1, N)
    def _(k):
        pl.semaphore_signal(
            barrier, inc=1, device_id={"ctx": lax.rem(me + k, N)}, device_id_type=MESH
        )

    @pl.loop(0, NG)
    def _(c):
        a, b = fetch_in(c, c)
        a.start()
        b.start()

    @pl.loop(0, ND)
    def _(c):
        fetch_out(c, c).start()

    ends = [lengths[0]]
    for i in range(1, 4):
        ends.append(ends[-1] + lengths[i])

    @pl.when(holds)
    def _():
        tok = me * 128 + lax.broadcasted_iota(jnp.int32, (128, 1), 0)
        prior = jnp.zeros((128, 1), jnp.int32)
        for i in range(4):
            prior = prior + jnp.where(tok >= ends[i], lengths[i], 0)
        places = old_angle.shape[0]
        pos = jnp.clip(tok - prior, 0, places - 1)
        pick = (lax.broadcasted_iota(jnp.int32, (128, places), 1) == pos).astype(f32).astype(bf16)
        d = new_angle[...] - old_angle[...]
        d1 = d.astype(bf16)
        rest = d - d1.astype(f32)
        d2 = rest.astype(bf16)
        d3 = (rest - d2.astype(f32)).astype(bf16)
        delta = dot(pick, d1) + dot(pick, d2) + dot(pick, d3)
        delta = jnp.concatenate([delta, delta], axis=1)
        lane = lax.broadcasted_iota(jnp.int32, (128, 128), 1)
        cosine = jnp.cos(delta)
        sine = jnp.sin(delta)
        sine = jnp.where(lane < HD // 2, -sine, sine)
        for j in range(KVH):
            k = old_cache[:, j * HD:(j + 1) * HD].astype(f32)
            kv[j, 0] = (k * cosine + pltpu.roll(k, HD // 2, 1) * sine).astype(bf16)
            kv[j, 1] = old_cache[:, (KVH + j) * HD:(KVH + j + 1) * HD]

    pl.semaphore_wait(barrier, N - 1)

    @pl.loop(1, N)
    def _(k):
        to = lax.rem(me + k, N)

        @pl.when(to < HOLD)
        def _():
            remote(pack.at[to], packr.at[me], p_s.at[to], p_r.at[me], to).start()

    @pl.when(holds)
    def _():
        @pl.loop(1, HOLD)
        def _(k):
            to = lax.rem(me + k, HOLD)
            remote(kv.at[to], kvr.at[me], kv_s.at[to], kv_r.at[me], to).start()

        packr[me] = pack[me]
        kvr[me] = kv[me]

        slot_l = slots[...]
        row_i = lax.broadcasted_iota(jnp.int32, (128, 128), 0)
        col_i = lax.broadcasted_iota(jnp.int32, (128, 128), 1)
        target_l = jnp.broadcast_to(lax.shift_right_arithmetic(slot_l, 6), (128, 128))
        target_s = jnp.sum(
            jnp.where(row_i == col_i, target_l, 0).astype(f32), axis=1, keepdims=True
        ).astype(jnp.int32)
        ahead = (target_s == target_l) & (row_i < col_i)
        rank = jnp.sum(ahead.astype(f32), axis=0, keepdims=True).astype(jnp.int32)
        dest = target_l * PEER + rank
        perm = (row_i == dest).astype(f32)
        place = jnp.sum(
            perm * jnp.bitwise_and(slot_l, CTOK_DEV - 1).astype(f32), axis=1, keepdims=True
        )
        perm = perm.astype(bf16)
        place = jnp.broadcast_to(place, (128, 128)).reshape(N, PEER, 128)
        sent[:, :, KVH * HD:] = jnp.concatenate([place, place], axis=1).astype(bf16)
        for j in range(KVH):
            ks = dot(perm, kv[j, 0]).reshape(N, PEER, HD)
            vs = dot(perm, kv[j, 1]).reshape(N, PEER, HD)
            sent[:, :, j * HD:(j + 1) * HD] = jnp.concatenate([ks, vs], axis=1).astype(bf16)

        @pl.loop(1, N)
        def _(k):
            frm = lax.rem(me + k, N)
            remote(pack.at[0], packr.at[frm], p_s.at[0], p_r.at[frm], frm).wait_recv()

        @pl.loop(1, HOLD)
        def _(k):
            frm = lax.rem(me + k, HOLD)
            remote(kv.at[0], kvr.at[frm], kv_s.at[0], kv_r.at[frm], frm).wait_recv()

        scale = 1.0 / float(HD) ** 0.5
        q = packr[:, 0:16].reshape(256, HD)
        k_own = packr[:, 16:32].reshape(256, HD)
        v_own = packr[:, 32:48].reshape(256, HD)
        k_all = kvr[:, 0].reshape(HOLD * 128, HD)
        v_all = kvr[:, 1].reshape(HOLD * 128, HD)
        s1 = dot(q, k_all, ((1,), (1,))) * scale
        s2 = dot(q, k_own, ((1,), (1,))) * scale
        tok = lax.broadcasted_iota(jnp.int32, (1, HOLD * 128), 1)
        row_of = jnp.zeros((1, HOLD * 128), jnp.int32)
        for i in range(4):
            row_of = row_of + (tok >= ends[i]).astype(jnp.int32)
        request = lax.broadcasted_iota(jnp.int32, (256, 1), 0) // 64
        s1 = jnp.where(request == row_of, s1, -1e30)
        qi = lax.broadcasted_iota(jnp.int32, (256, 256), 0)
        ni = lax.broadcasted_iota(jnp.int32, (256, 256), 1)
        mine = (qi // 16 == ni // 16) & (ni % 16 <= (qi % 16) // 8)
        s2 = jnp.where(mine, s2, -1e30)
        top = jnp.maximum(
            jnp.max(s1, axis=1, keepdims=True), jnp.max(s2, axis=1, keepdims=True)
        )
        w1 = jnp.exp(s1 - top)
        w2 = jnp.exp(s2 - top)
        total = jnp.sum(w1, axis=1, keepdims=True) + jnp.sum(w2, axis=1, keepdims=True)
        res = (split_dot(w1, v_all) + split_dot(w2, v_own)) / total
        attn[...] = res.reshape(N, ROWS, HD)
        attnr[me] = attn[me]

        @pl.loop(1, N)
        def _(k):
            to = lax.rem(me + k, N)
            remote(attn.at[to], attnr.at[me], a_s.at[to], a_r.at[me], to).start()

    @pl.loop(0, HOLD)
    def _(frm):
        @pl.when(frm != me)
        def _():
            other = lax.rem(me + 1, N)
            remote(attn.at[0], attnr.at[frm], a_s.at[0], a_r.at[frm], other).wait_recv()

    h = resid[...].astype(f32) + attnr[...]
    hst[...] = h
    h4 = h.reshape(KVH, 2, GROUP, HD)
    sq = jnp.sum(jnp.sum(h4 * h4, axis=0), axis=-1, keepdims=True)
    mean = jnp.sum(sq, axis=1, keepdims=True) / float(KVH * GROUP * HD)
    inv = lax.rsqrt(mean + 1e-05)
    normed = h4 * inv[None] * gain[...].astype(f32).reshape(KVH, 1, GROUP, HD)
    norm[me] = normed.reshape(KVH, ROWS, HD).astype(bf16)

    z, x, core = me // 4, lax.rem(me // 2, 2), lax.rem(me, 2)

    def at(zz, xx, cc):
        return zz * 4 + xx * 2 + cc

    x_peer, c_peer = at(z, 1 - x, core), at(z, x, 1 - core)

    def push(block, sem, to):
        return remote(norm.at[block], norm.at[block], n_s.at[sem], n_r.at[block], to)

    for i in range(1, 4):
        push(me, i - 1, at(lax.rem(z + i, 4), x, core)).start()
    push(me, 3, x_peer).start()
    push(me, 4, c_peer).start()
    for i in range(1, 4):
        block = at(lax.rem(z + i, 4), x, core)
        push(block, 0, x_peer).wait_recv()
        push(block, 3 + 2 * i, x_peer).start()
        push(block, 4 + 2 * i, c_peer).start()
    for i in range(4):
        block = at(lax.rem(z + i, 4), 1 - x, core)
        push(block, 0, x_peer).wait_recv()
        push(block, 11 + i, c_peer).start()

    @pl.loop(0, N // 2)
    def _(i):
        push(i * 2 + 1 - core, 0, x_peer).wait_recv()

    @pl.when(holds)
    def _():
        @pl.loop(1, N)
        def _(k):
            to = lax.rem(me + k, N)
            remote(sent.at[to], got.at[me], t_s.at[to], t_r.at[me], to).start()

        got[me] = sent[me]

    for j in range(KVH):
        wide[...] = norm[:, j].reshape(256, HD).astype(f32)
        for g in range(GROUP):
            part = wide[pl.ds(g, 32, stride=GROUP), :].astype(bf16)
            xs[2 * j + g // 4, :, (g % 4) * HD:(g % 4 + 1) * HD] = part

    accg[...] = jnp.zeros_like(accg)
    accu[...] = jnp.zeros_like(accu)

    @pl.loop(0, steps)
    def _(c):
        s = lax.rem(c, NG)
        a, b = fetch_in(c, s)
        a.wait()
        accg[...] += dot(xs[c], wg[s])
        b.wait()
        accu[...] += dot(xs[c], wu[s])

        @pl.when(c + NG < steps)
        def _():
            a2, b2 = fetch_in(c + NG, s)
            a2.start()
            b2.start()

    gate = accg[...]
    hidden[...] = (gate / (1.0 + jnp.exp(-gate)) * accu[...]).astype(bf16)

    def give(c, to):
        return remote(
            sbuf.at[c, to], rbuf.at[c, me], f_s.at[c, to], f_r.at[c, me], to
        )

    @pl.loop(0, dsteps)
    def _(c):
        s = lax.rem(c, ND)
        fetch_out(c, s).wait()
        part = dot(hidden[...], wd[s])
        for g in range(GROUP):
            obuf[pl.ds(g, 32, stride=GROUP), :] = part[:, g * HD:(g + 1) * HD]
        sbuf[c] = obuf[...].reshape(N, ROWS, HD).astype(bf16)

        @pl.when(c + ND < dsteps)
        def _():
            fetch_out(c + ND, s).start()

        rbuf[c, me] = sbuf[c, me]

        @pl.loop(1, N)
        def _(k):
            give(c, lax.rem(me + k, N)).start()

    @pl.loop(0, HOLD)
    def _(frm):
        @pl.when(frm != me)
        def _():
            other = lax.rem(me + 1, N)
            remote(sent.at[0], got.at[frm], t_s.at[0], t_r.at[frm], other).wait_recv()

    rows = HOLD * PEER
    where = got[:, :, KVH * HD:].astype(f32)[:, 0:PEER].reshape(rows, 128)
    lane = lax.broadcasted_iota(jnp.int32, (rows, 128), 1).astype(f32)
    put = (where == lane).astype(f32).astype(bf16)
    for j in range(KVH):
        both = got[:, :, j * HD:(j + 1) * HD].astype(f32)
        ks = both[:, 0:PEER].reshape(rows, HD).astype(bf16)
        vs = both[:, PEER:].reshape(rows, HD).astype(bf16)
        new_k = dot(put, ks, ((0,), (0,)))[0:CTOK_DEV]
        new_v = dot(put, vs, ((0,), (0,)))[0:CTOK_DEV]
        new_cache[:, j * HD:(j + 1) * HD] = new_k.astype(bf16)
        new_cache[:, (KVH + j) * HD:(KVH + j + 1) * HD] = new_v.astype(bf16)

    @pl.loop(0, dsteps)
    def _(c):
        @pl.loop(1, N)
        def _(k):
            frm = lax.rem(me + k, N)
            remote(
                sbuf.at[0, 0], rbuf.at[c, frm], f_s.at[0, 0], f_r.at[c, frm], frm
            ).wait_recv()

        out[c] = (hst[c] + jnp.sum(rbuf[c].astype(f32), axis=0)).astype(bf16)

    @pl.loop(1, N)
    def _(k):
        to = lax.rem(me + k, N)

        @pl.when(to < HOLD)
        def _():
            remote(pack.at[to], packr.at[me], p_s.at[to], p_r.at[me], to).wait_send()

        @pl.loop(0, dsteps)
        def _(c):
            give(c, to).wait_send()

    @pl.when(holds)
    def _():
        @pl.loop(1, HOLD)
        def _(k):
            to = lax.rem(me + k, HOLD)
            remote(kv.at[to], kvr.at[me], kv_s.at[to], kv_r.at[me], to).wait_send()

        @pl.loop(1, N)
        def _(k):
            to = lax.rem(me + k, N)
            remote(attn.at[to], attnr.at[me], a_s.at[to], a_r.at[me], to).wait_send()
            remote(sent.at[to], got.at[me], t_s.at[to], t_r.at[me], to).wait_send()

    @pl.loop(0, 15)
    def _(i):
        push(me, i, x_peer).wait_send()


def fused(
    old_cache, new_slot, lengths, old_angle, new_angle, queries, new_kv, resid, gain,
    w_gate, w_up, w_down,
):
    bf16, f32 = jnp.bfloat16, jnp.float32
    width = w_gate.shape[1]
    model = w_gate.shape[0]

    def by_head(a):
        return a.reshape(2, KVH, GROUP, HD).transpose(1, 0, 2, 3).reshape(KVH, ROWS, HD)

    own = new_kv.reshape(2, 2, KVH, HD).transpose(1, 2, 0, 3)
    own = jnp.pad(own, ((0, 0), (0, 0), (0, ROWS - 2), (0, 0)))
    pack = jnp.concatenate([by_head(queries), own[0], own[1]], axis=1)
    vmem = pl.BlockSpec(memory_space=pltpu.VMEM)
    smem = pl.BlockSpec(memory_space=pltpu.SMEM)
    hbm = pl.BlockSpec(memory_space=pl.ANY)
    dma = pltpu.SemaphoreType.DMA
    dsteps = model // DC
    new_cache, out = pl.pallas_call(
        kernel,
        out_shape=(
            jax.ShapeDtypeStruct((CTOK_DEV, old_cache.shape[1]), bf16),
            jax.ShapeDtypeStruct((KVH, ROWS, HD), bf16),
        ),
        in_specs=[vmem, vmem, smem, vmem, vmem, vmem, vmem, vmem, hbm, hbm, hbm],
        out_specs=(vmem, vmem),
        scratch_shapes=[
            pltpu.VMEM((NG, KC, width), bf16),
            pltpu.VMEM((NG, KC, width), bf16),
            pltpu.VMEM((ND, width, DC), bf16),
            pltpu.VMEM((KVH, 2, 128, HD), bf16),
            pltpu.VMEM((HOLD, 2, 128, HD), bf16),
            pltpu.VMEM((N, 48, HD), bf16),
            pltpu.VMEM((N, ROWS, (KVH + 1) * HD), bf16),
            pltpu.VMEM((HOLD, ROWS, (KVH + 1) * HD), bf16),
            pltpu.VMEM((N, ROWS, HD), f32),
            pltpu.VMEM((KVH, ROWS, HD), f32),
            pltpu.VMEM((N, KVH, ROWS, HD), bf16),
            pltpu.VMEM((256, HD), f32),
            pltpu.VMEM((model // KC, 32, KC), bf16),
            pltpu.VMEM((32, width), f32),
            pltpu.VMEM((32, width), f32),
            pltpu.VMEM((32, width), bf16),
            pltpu.VMEM((256, HD), f32),
            pltpu.VMEM((dsteps, N, ROWS, HD), bf16),
            pltpu.VMEM((dsteps, N, ROWS, HD), bf16),
            pltpu.VMEM((KVH, ROWS, HD), f32),
            dma((NG,)), dma((NG,)), dma((ND,)),
            dma((HOLD,)), dma((HOLD,)),
            dma((N,)), dma((N,)),
            dma((N,)), dma((HOLD,)),
            dma((15,)), dma((N,)),
            dma((N,)), dma((HOLD,)),
            dma((dsteps, N)), dma((dsteps, N)),
        ],
        compiler_params=pltpu.CompilerParams(
            collective_id=0, has_side_effects=True, vmem_limit_bytes=60 * 1024 * 1024
        ),
    )(
        old_cache, new_slot.reshape(1, -1), lengths, old_angle, new_angle, pack,
        by_head(resid), gain.reshape(KVH, GROUP, HD), w_gate, w_up, w_down,
    )
    out = out.reshape(KVH, 2, GROUP, HD).transpose(1, 0, 2, 3).reshape(2, model)
    return new_cache, out


def rotate_block(block, where_pos, old_angle, new_angle):
    rows_here = block.shape[0]
    half_size = HD // 2
    parts = block.reshape(rows_here, 2, KVH, HD)
    keys = parts[:, 0].astype(jnp.float32)
    delta = jnp.take(new_angle, where_pos, axis=0) - jnp.take(old_angle, where_pos, axis=0)
    cosine = jnp.cos(delta)[:, None, :]
    sine = jnp.sin(delta)[:, None, :]
    first = keys[..., :half_size]
    second = keys[..., half_size:]
    turned = jnp.concatenate(
        [first * cosine - second * sine, second * cosine + first * sine], axis=-1
    ).astype(jnp.bfloat16)
    return jnp.stack([turned, parts[:, 1]], axis=1).reshape(rows_here, 2 * KVH * HD)


def per_device(
    old_cache,
    new_slot,
    lengths,
    old_angle,
    new_angle,
    queries,
    new_kv,
    resid,
    gain,
    w_gate,
    w_up,
    w_down,
):
    devices = lax.axis_size("ctx")
    own_index = lax.axis_index("ctx")
    slot_count = old_cache.shape[0]
    row_width = old_cache.shape[1]
    per_peer = slot_count // devices
    rows_dev = queries.shape[0]
    all_rows = rows_dev * devices
    group_size = QH // KVH
    high = lax.Precision.HIGHEST
    scale = 1.0 / float(HD) ** 0.5
    tokens = own_index * slot_count + jnp.arange(slot_count, dtype=jnp.int32)
    requests = jnp.arange(lengths.shape[0], dtype=jnp.int32)
    row_ends = jnp.sum(jnp.where(requests[None, :] <= requests[:, None], lengths[None, :], 0), axis=1)
    passed = row_ends[None, :] <= tokens[:, None]
    owner_row = jnp.minimum(jnp.sum(passed.astype(jnp.int32), axis=1), lengths.shape[0] - 1)
    row_prior = jnp.sum(jnp.where(passed, lengths[None, :], 0), axis=1)
    position = jnp.clip(tokens - row_prior, 0, old_angle.shape[0] - 1)
    filled = new_slot >= 0
    all_queries = lax.all_gather(queries, "ctx", axis=0, tiled=True)
    target = jnp.where(
        filled, new_slot // CTOK_DEV, jnp.arange(slot_count, dtype=jnp.int32) // per_peer
    )
    sorted_order = jnp.argsort(target, stable=True)
    new_place = jnp.where(filled, new_slot % CTOK_DEV, -1)
    slot_info = jnp.stack([new_place, owner_row, position], axis=1)[sorted_order]
    sent_rows = old_cache[sorted_order].reshape(devices, per_peer, row_width)
    got_rows = lax.all_to_all(sent_rows, "ctx", split_axis=0, concat_axis=0, tiled=True)
    got_info = lax.all_to_all(
        slot_info.reshape(devices, per_peer, 3), "ctx", split_axis=0, concat_axis=0, tiled=True
    )
    got_rows = got_rows.reshape(slot_count, row_width)
    got_info = got_info.reshape(slot_count, 3)
    landing = jnp.where(got_info[:, 0] >= 0, got_info[:, 0], CTOK_DEV)
    placed = jnp.zeros((CTOK_DEV, row_width), jnp.bfloat16).at[landing].set(got_rows, mode="drop")
    placed_row = jnp.zeros((CTOK_DEV,), jnp.int32).at[landing].set(got_info[:, 1], mode="drop")
    placed_pos = jnp.zeros((CTOK_DEV,), jnp.int32).at[landing].set(got_info[:, 2], mode="drop")
    placed, moved_row, moved_pos = (placed, placed_row, placed_pos)
    new_cache = rotate_block(placed, moved_pos, old_angle, new_angle)
    key_count = new_cache.shape[0]
    key_split = new_cache.reshape(key_count, 2, KVH, HD)
    value_four = key_split[:, 1].astype(jnp.float32)
    query_four = all_queries.reshape(all_rows, KVH, group_size, HD)
    scores = (
        jnp.einsum(
            "mjge,cje->mjgc", query_four, key_split[:, 0], preferred_element_type=jnp.float32
        )
        * scale
    )
    query_row = jnp.arange(all_rows, dtype=jnp.int32) // (2 * SAMPLES)
    matching = query_row[:, None] == moved_row[None, :]
    scores = jnp.where(matching[:, None, None, :], scores, -1e30)
    local_top = jnp.max(scores, axis=-1)
    own_query = queries.reshape(rows_dev, KVH, group_size, HD).astype(jnp.float32)
    fresh_kv = jnp.repeat(new_kv.reshape(rows_dev // 2, 2, 2, KVH, HD), 2, axis=0).astype(
        jnp.float32
    )
    own_steps = (
        jnp.arange(2, dtype=jnp.int32)[None, :]
        <= (jnp.arange(rows_dev, dtype=jnp.int32) % 2)[:, None]
    )
    own_scores = jnp.einsum("mjge,msje->mjgs", own_query, fresh_kv[:, :, 0], precision=high) * scale
    own_scores = jnp.where(own_steps[:, None, None, :], own_scores, -1e30)
    own_top = jnp.max(own_scores, axis=-1)
    floor_top = jnp.maximum(local_top, -10000.0)
    weights_local = jnp.exp(scores - floor_top[..., None])
    summed = jnp.einsum("mjgc,cje->mjge", weights_local, value_four, precision=high)
    totals = jnp.sum(weights_local, axis=-1)
    got_sums, got_totals, got_tops = (
        lax.all_to_all(
            summed.reshape(devices, rows_dev, QH * HD),
            "ctx",
            split_axis=0,
            concat_axis=0,
            tiled=True,
        ),
        lax.all_to_all(
            totals.reshape(devices, rows_dev, QH), "ctx", split_axis=0, concat_axis=0, tiled=True
        ),
        lax.all_to_all(
            floor_top.reshape(devices, rows_dev, QH), "ctx", split_axis=0, concat_axis=0, tiled=True
        ),
    )
    got_tops = got_tops.reshape(devices, rows_dev, KVH, group_size)
    row_top = jnp.maximum(jnp.max(got_tops, axis=0), own_top)
    rescale = jnp.exp(got_tops - row_top[None])
    weights_own = jnp.exp(own_scores - row_top[..., None])
    row_sums = jnp.sum(
        rescale[..., None] * got_sums.reshape(devices, rows_dev, KVH, group_size, HD), axis=0
    )
    row_sums = row_sums + jnp.einsum(
        "mjgs,msje->mjge", weights_own, fresh_kv[:, :, 1], precision=high
    )
    row_totals = jnp.sum(
        rescale * got_totals.reshape(devices, rows_dev, KVH, group_size), axis=0
    ) + jnp.sum(weights_own, axis=-1)
    attn = (row_sums / row_totals[..., None]).reshape(rows_dev, QH * HD)
    hstate = resid.astype(jnp.float32) + attn
    normed = (
        hstate
        * lax.rsqrt(jnp.mean(hstate * hstate, axis=-1, keepdims=True) + 1e-05)
        * gain.astype(jnp.float32)
    ).astype(jnp.bfloat16)
    piece = lax.all_gather(normed, "ctx", axis=0, tiled=True)
    gate_out = jnp.dot(piece, w_gate, preferred_element_type=jnp.float32)
    up_out = jnp.dot(piece, w_up, preferred_element_type=jnp.float32)
    hidden_all = (jax.nn.silu(gate_out) * up_out).astype(jnp.bfloat16)
    ffn_out = lax.psum_scatter(
        jnp.dot(hidden_all, w_down, preferred_element_type=jnp.float32),
        "ctx",
        scatter_dimension=0,
        tiled=True,
    )
    layer_out = (hstate + ffn_out).astype(jnp.bfloat16)
    return (new_cache, layer_out)


def solution(mesh):
    return jax.shard_map(
        fused if mesh.shape["ctx"] == N else per_device,
        mesh=mesh,
        in_specs=(
            P(("groups", "ctx"), None),
            P(("groups", "ctx")),
            P("groups"),
            P(),
            P(),
            P(("groups", "ctx"), None),
            P(("groups", "ctx"), None),
            P(("groups", "ctx"), None),
            P(),
            P(None, "ctx"),
            P(None, "ctx"),
            P("ctx", None),
        ),
        out_specs=(P(("groups", "ctx"), None), P(("groups", "ctx"), None)),
        check_vma=False,
    )
```

```python
import jax
import jax.numpy as jnp
from jax import lax
from jax.experimental import pallas as pl
from jax.experimental.pallas import tpu as pltpu
from jax.sharding import PartitionSpec as P

QH = 64
KVH = 8
HD = 128
CTOK_DEV = 64
SAMPLES = 4

N = 16
HOLD = 8
PEER = 8
GROUP = QH // KVH
ROWS = 16
KC = 512
NG = 11
DC = 1024
ND = 3
MESH = pl.DeviceIdType.MESH


def remote(src, dst, send_sem, recv_sem, dev):
    return pltpu.make_async_remote_copy(
        src_ref=src,
        dst_ref=dst,
        send_sem=send_sem,
        recv_sem=recv_sem,
        device_id={"ctx": dev},
        device_id_type=MESH,
    )


def dot(a, b, dims=((1,), (0,))):
    return lax.dot_general(a, b, (dims, ((), ())), preferred_element_type=jnp.float32)


def split_dot(a, b):
    hi = a.astype(jnp.bfloat16)
    lo = (a - hi.astype(jnp.float32)).astype(jnp.bfloat16)
    return dot(hi, b) + dot(lo, b)


def kernel(
    old_cache, slots, lengths, old_angle, new_angle, queries, own_kv, resid, gain,
    w_gate, w_up, w_down,
    new_cache, out,
    packf, pack, tall,
    wg, wu, wd, kv, kvr, packr, sent, got, attn, attnr, norm, wide, xs, accg, accu,
    hidden, obuf, sbuf, rbuf, hst,
    g_sem, u_sem, d_sem, kv_s, kv_r, p_s, p_r, a_s, a_r, n_s, n_r, t_s, t_r, f_s, f_r,
):
    f32, bf16 = jnp.float32, jnp.bfloat16
    me = lax.axis_index("ctx")
    steps = w_gate.shape[0] // KC
    dsteps = w_down.shape[1] // DC
    holds = me < HOLD

    def fetch_in(c, s):
        rows = pl.ds(pl.multiple_of(c * KC, KC), KC)
        return (
            pltpu.make_async_copy(w_gate.at[rows, :], wg.at[s], g_sem.at[s]),
            pltpu.make_async_copy(w_up.at[rows, :], wu.at[s], u_sem.at[s]),
        )

    def fetch_out(c, s):
        cols = pl.ds(pl.multiple_of(c * DC, DC), DC)
        return pltpu.make_async_copy(w_down.at[:, cols], wd.at[s], d_sem.at[s])

    barrier = pltpu.get_barrier_semaphore()

    @pl.loop(1, N)
    def _(k):
        pl.semaphore_signal(
            barrier, inc=1, device_id={"ctx": lax.rem(me + k, N)}, device_id_type=MESH
        )

    @pl.loop(0, NG)
    def _(c):
        a, b = fetch_in(c, c)
        a.start()
        b.start()

    @pl.loop(0, ND)
    def _(c):
        fetch_out(c, c).start()

    packf[...] = jnp.zeros_like(packf)
    for j in range(KVH):
        for g in range(GROUP):
            cols = slice((j * GROUP + g) * HD, (j * GROUP + g + 1) * HD)
            packf[j, pl.ds(g, 2, stride=GROUP), :] = queries[:, cols].astype(f32)
        packf[j, 16:18, :] = own_kv[:, j * HD:(j + 1) * HD].astype(f32)
        packf[j, 32:34, :] = own_kv[:, (KVH + j) * HD:(KVH + j + 1) * HD].astype(f32)
    pack[...] = packf[...].astype(bf16)

    ends = [lengths[0]]
    for i in range(1, 4):
        ends.append(ends[-1] + lengths[i])

    @pl.when(holds)
    def _():
        tok = me * 128 + lax.broadcasted_iota(jnp.int32, (128, 1), 0)
        prior = jnp.zeros((128, 1), jnp.int32)
        for i in range(4):
            prior = prior + jnp.where(tok >= ends[i], lengths[i], 0)
        places = old_angle.shape[1]
        pos = jnp.clip(tok - prior, 0, places - 1)
        pick = (lax.broadcasted_iota(jnp.int32, (128, places), 1) == pos).astype(f32).astype(bf16)
        d = new_angle[...] - old_angle[...]
        d1 = d.astype(bf16)
        rest = d - d1.astype(f32)
        d2 = rest.astype(bf16)
        d3 = (rest - d2.astype(f32)).astype(bf16)
        last = ((1,), (1,))
        delta = dot(pick, d1, last) + dot(pick, d2, last) + dot(pick, d3, last)
        delta = jnp.concatenate([delta, delta], axis=1)
        lane = lax.broadcasted_iota(jnp.int32, (128, 128), 1)
        cosine = jnp.cos(delta)
        sine = jnp.sin(delta)
        sine = jnp.where(lane < HD // 2, -sine, sine)
        for j in range(KVH):
            k = old_cache[:, j * HD:(j + 1) * HD].astype(f32)
            kv[j, 0] = (k * cosine + pltpu.roll(k, HD // 2, 1) * sine).astype(bf16)
            kv[j, 1] = old_cache[:, (KVH + j) * HD:(KVH + j + 1) * HD]

    pl.semaphore_wait(barrier, N - 1)

    @pl.loop(1, N)
    def _(k):
        to = lax.rem(me + k, N)

        @pl.when(to < HOLD)
        def _():
            remote(pack.at[to], packr.at[me], p_s.at[to], p_r.at[0], to).start()

    @pl.when(holds)
    def _():
        @pl.loop(1, HOLD)
        def _(k):
            to = lax.rem(me + k, HOLD)
            remote(kv.at[to], kvr.at[me], kv_s.at[to], kv_r.at[me], to).start()

        packr[me] = pack[me]
        kvr[me] = kv[me]

        slot_l = slots[...]
        row_i = lax.broadcasted_iota(jnp.int32, (128, 128), 0)
        col_i = lax.broadcasted_iota(jnp.int32, (128, 128), 1)
        target_l = jnp.broadcast_to(lax.shift_right_arithmetic(slot_l, 6), (128, 128))
        target_s = jnp.sum(
            jnp.where(row_i == col_i, target_l, 0).astype(f32), axis=1, keepdims=True
        ).astype(jnp.int32)
        ahead = (target_s == target_l) & (row_i < col_i)
        rank = jnp.sum(ahead.astype(f32), axis=0, keepdims=True).astype(jnp.int32)
        dest = target_l * PEER + rank
        perm = (row_i == dest).astype(f32)
        place = jnp.sum(
            perm * jnp.bitwise_and(slot_l, CTOK_DEV - 1).astype(f32), axis=1, keepdims=True
        )
        perm = perm.astype(bf16)
        place = jnp.broadcast_to(place, (128, 128)).reshape(N, PEER, 128)
        sent[:, :, KVH * HD:] = jnp.concatenate([place, place], axis=1).astype(bf16)
        for j in range(KVH):
            ks = dot(perm, kv[j, 0]).reshape(N, PEER, HD)
            vs = dot(perm, kv[j, 1]).reshape(N, PEER, HD)
            sent[:, :, j * HD:(j + 1) * HD] = jnp.concatenate([ks, vs], axis=1).astype(bf16)

        rest15 = packr.at[pl.ds(0, N - 1)]
        remote(rest15, rest15, p_s.at[0], p_r.at[0], lax.rem(me + 1, N)).wait_recv()

        @pl.loop(1, HOLD)
        def _(k):
            frm = lax.rem(me + k, HOLD)
            remote(kv.at[0], kvr.at[frm], kv_s.at[0], kv_r.at[frm], frm).wait_recv()

        scale = 1.0 / float(HD) ** 0.5
        q = packr[:, 0:16].reshape(256, HD)
        k_own = packr[:, 16:32].reshape(256, HD)
        v_own = packr[:, 32:48].reshape(256, HD)
        k_all = kvr[:, 0].reshape(HOLD * 128, HD)
        v_all = kvr[:, 1].reshape(HOLD * 128, HD)
        s1 = dot(q, k_all, ((1,), (1,))) * scale
        s2 = dot(q, k_own, ((1,), (1,))) * scale
        tok = lax.broadcasted_iota(jnp.int32, (1, HOLD * 128), 1)
        row_of = jnp.zeros((1, HOLD * 128), jnp.int32)
        for i in range(4):
            row_of = row_of + (tok >= ends[i]).astype(jnp.int32)
        request = lax.broadcasted_iota(jnp.int32, (256, 1), 0) // 64
        s1 = jnp.where(request == row_of, s1, -1e30)
        qi = lax.broadcasted_iota(jnp.int32, (256, 256), 0)
        ni = lax.broadcasted_iota(jnp.int32, (256, 256), 1)
        mine = (qi // 16 == ni // 16) & (ni % 16 <= (qi % 16) // 8)
        s2 = jnp.where(mine, s2, -1e30)
        top = jnp.maximum(
            jnp.max(s1, axis=1, keepdims=True), jnp.max(s2, axis=1, keepdims=True)
        )
        w1 = jnp.exp(s1 - top)
        w2 = jnp.exp(s2 - top)
        total = jnp.sum(w1, axis=1, keepdims=True) + jnp.sum(w2, axis=1, keepdims=True)
        res = (split_dot(w1, v_all) + split_dot(w2, v_own)) / total
        attn[...] = res.reshape(N, ROWS, HD)
        attnr[me] = attn[me]

        @pl.loop(1, N)
        def _(k):
            to = lax.rem(me + k, N)
            remote(attn.at[to], attnr.at[me], a_s.at[0], a_r.at[me], to).start()

    for j in range(KVH):
        for g in range(GROUP):
            cols = slice((j * GROUP + g) * HD, (j * GROUP + g + 1) * HD)
            tall[0, j, pl.ds(g, 2, stride=GROUP), :] = resid[:, cols].astype(f32)
            tall[1, j, pl.ds(g, 2, stride=GROUP), :] = jnp.broadcast_to(
                gain[:, cols].astype(f32), (2, HD)
            )

    @pl.loop(0, HOLD)
    def _(frm):
        @pl.when(frm != me)
        def _():
            other = lax.rem(me + 1, N)
            remote(attn.at[0], attnr.at[frm], a_s.at[0], a_r.at[frm], other).wait_recv()

    h = tall[0] + attnr[...]
    hst[...] = h
    h4 = h.reshape(KVH, 2, GROUP, HD)
    sq = jnp.sum(jnp.sum(h4 * h4, axis=0), axis=-1, keepdims=True)
    mean = jnp.sum(sq, axis=1, keepdims=True) / float(KVH * GROUP * HD)
    inv = lax.rsqrt(mean + 1e-05)
    normed = h4 * inv[None] * tall[1].reshape(KVH, 2, GROUP, HD)
    norm[me] = normed.reshape(KVH, ROWS, HD).astype(bf16)

    z, x, core = me // 4, lax.rem(me // 2, 2), lax.rem(me, 2)

    def at(zz, xx, cc):
        return zz * 4 + xx * 2 + cc

    x_peer, c_peer = at(z, 1 - x, core), at(z, x, 1 - core)

    def push(block, sem, to):
        return remote(norm.at[block], norm.at[block], n_s.at[sem], n_r.at[block], to)

    for i in range(1, 4):
        push(me, i - 1, at(lax.rem(z + i, 4), x, core)).start()
    push(me, 3, x_peer).start()
    push(me, 4, c_peer).start()
    for i in range(1, 4):
        block = at(lax.rem(z + i, 4), x, core)
        push(block, 0, x_peer).wait_recv()
        push(block, 3 + 2 * i, x_peer).start()
        push(block, 4 + 2 * i, c_peer).start()
    for i in range(4):
        block = at(lax.rem(z + i, 4), 1 - x, core)
        push(block, 0, x_peer).wait_recv()
        push(block, 11 + i, c_peer).start()

    @pl.loop(0, N // 2)
    def _(i):
        push(i * 2 + 1 - core, 0, x_peer).wait_recv()

    @pl.when(holds)
    def _():
        @pl.loop(1, N)
        def _(k):
            to = lax.rem(me + k, N)
            remote(sent.at[to], got.at[me], t_s.at[0], t_r.at[me], to).start()

        got[me] = sent[me]

    for j in range(KVH):
        wide[...] = norm[:, j].reshape(256, HD).astype(f32)
        for g in range(GROUP):
            part = wide[pl.ds(g, 32, stride=GROUP), :].astype(bf16)
            xs[2 * j + g // 4, :, (g % 4) * HD:(g % 4 + 1) * HD] = part

    accg[...] = jnp.zeros_like(accg)
    accu[...] = jnp.zeros_like(accu)

    @pl.loop(0, steps)
    def _(c):
        s = lax.rem(c, NG)
        a, b = fetch_in(c, s)
        a.wait()
        accg[...] += dot(xs[c], wg[s])
        b.wait()
        accu[...] += dot(xs[c], wu[s])

        @pl.when(c + NG < steps)
        def _():
            a2, b2 = fetch_in(c + NG, s)
            a2.start()
            b2.start()

    gate = accg[...]
    hidden[...] = (gate / (1.0 + jnp.exp(-gate)) * accu[...]).astype(bf16)

    def give(p, to):
        two = pl.ds(2 * p, 2)
        return remote(sbuf.at[two, to], rbuf.at[two, me], f_s.at[p], f_r.at[p], to)

    def given(p):
        two, some = pl.ds(2 * p, 2), pl.ds(0, N - 1)
        return remote(
            sbuf.at[two, some], rbuf.at[two, some], f_s.at[p], f_r.at[p], lax.rem(me + 1, N)
        )

    @pl.loop(0, dsteps)
    def _(c):
        s = lax.rem(c, ND)
        fetch_out(c, s).wait()
        part = dot(hidden[...], wd[s])
        for g in range(GROUP):
            obuf[pl.ds(g, 32, stride=GROUP), :] = part[:, g * HD:(g + 1) * HD]
        sbuf[c] = obuf[...].reshape(N, ROWS, HD).astype(bf16)

        @pl.when(c + ND < dsteps)
        def _():
            fetch_out(c + ND, s).start()

        rbuf[c, me] = sbuf[c, me]

        @pl.when(lax.rem(c, 2) == 1)
        def _():
            @pl.loop(1, N)
            def _(k):
                give(c // 2, lax.rem(me + k, N)).start()

    @pl.loop(0, HOLD)
    def _(frm):
        @pl.when(frm != me)
        def _():
            other = lax.rem(me + 1, N)
            remote(sent.at[0], got.at[frm], t_s.at[0], t_r.at[frm], other).wait_recv()

    rows = HOLD * PEER
    where = got[:, :, KVH * HD:].astype(f32)[:, 0:PEER].reshape(rows, 128)
    lane = lax.broadcasted_iota(jnp.int32, (rows, 128), 1).astype(f32)
    put = (where == lane).astype(f32).astype(bf16)
    for j in range(KVH):
        both = got[:, :, j * HD:(j + 1) * HD].astype(f32)
        ks = both[:, 0:PEER].reshape(rows, HD).astype(bf16)
        vs = both[:, PEER:].reshape(rows, HD).astype(bf16)
        new_k = dot(put, ks, ((0,), (0,)))[0:CTOK_DEV]
        new_v = dot(put, vs, ((0,), (0,)))[0:CTOK_DEV]
        new_cache[:, j * HD:(j + 1) * HD] = new_k.astype(bf16)
        new_cache[:, (KVH + j) * HD:(KVH + j + 1) * HD] = new_v.astype(bf16)

    for p in range(dsteps // 2):
        given(p).wait_recv()
        for c in (2 * p, 2 * p + 1):
            hst[c] = hst[c] + jnp.sum(rbuf[c].astype(f32), axis=0)
            for g in range(GROUP):
                cols = slice((c * GROUP + g) * HD, (c * GROUP + g + 1) * HD)
                out[:, cols] = hst[c, pl.ds(g, 2, stride=GROUP), :].astype(bf16)

    @pl.loop(1, N)
    def _(k):
        to = lax.rem(me + k, N)

        @pl.when(to < HOLD)
        def _():
            remote(pack.at[to], packr.at[me], p_s.at[to], p_r.at[0], to).wait_send()

    for p in range(dsteps // 2):
        given(p).wait_send()

    @pl.when(holds)
    def _():
        @pl.loop(1, HOLD)
        def _(k):
            to = lax.rem(me + k, HOLD)
            remote(kv.at[to], kvr.at[me], kv_s.at[to], kv_r.at[me], to).wait_send()

        other = lax.rem(me + 1, N)
        out_a, out_t = attn.at[pl.ds(0, N - 1)], sent.at[pl.ds(0, N - 1)]
        remote(out_a, out_a, a_s.at[0], a_r.at[me], other).wait_send()
        remote(out_t, out_t, t_s.at[0], t_r.at[me], other).wait_send()

    @pl.loop(0, 15)
    def _(i):
        push(me, i, x_peer).wait_send()


def fused(
    old_cache, new_slot, lengths, old_angle, new_angle, queries, new_kv, resid, gain,
    w_gate, w_up, w_down,
):
    bf16, f32 = jnp.bfloat16, jnp.float32
    width = w_gate.shape[1]
    model = w_gate.shape[0]

    vmem = pl.BlockSpec(memory_space=pltpu.VMEM)
    smem = pl.BlockSpec(memory_space=pltpu.SMEM)
    hbm = pl.BlockSpec(memory_space=pl.ANY)
    dma = pltpu.SemaphoreType.DMA
    dsteps = model // DC
    new_cache, out = pl.pallas_call(
        kernel,
        out_shape=(
            jax.ShapeDtypeStruct((CTOK_DEV, old_cache.shape[1]), bf16),
            jax.ShapeDtypeStruct((2, model), bf16),
        ),
        in_specs=[vmem, vmem, smem, vmem, vmem, vmem, vmem, vmem, vmem, hbm, hbm, hbm],
        out_specs=(vmem, vmem),
        scratch_shapes=[
            pltpu.VMEM((KVH, 48, HD), f32),
            pltpu.VMEM((KVH, 48, HD), bf16),
            pltpu.VMEM((2, KVH, ROWS, HD), f32),
            pltpu.VMEM((NG, KC, width), bf16),
            pltpu.VMEM((NG, KC, width), bf16),
            pltpu.VMEM((ND, width, DC), bf16),
            pltpu.VMEM((KVH, 2, 128, HD), bf16),
            pltpu.VMEM((HOLD, 2, 128, HD), bf16),
            pltpu.VMEM((N, 48, HD), bf16),
            pltpu.VMEM((N, ROWS, (KVH + 1) * HD), bf16),
            pltpu.VMEM((HOLD, ROWS, (KVH + 1) * HD), bf16),
            pltpu.VMEM((N, ROWS, HD), f32),
            pltpu.VMEM((KVH, ROWS, HD), f32),
            pltpu.VMEM((N, KVH, ROWS, HD), bf16),
            pltpu.VMEM((256, HD), f32),
            pltpu.VMEM((model // KC, 32, KC), bf16),
            pltpu.VMEM((32, width), f32),
            pltpu.VMEM((32, width), f32),
            pltpu.VMEM((32, width), bf16),
            pltpu.VMEM((256, HD), f32),
            pltpu.VMEM((dsteps, N, ROWS, HD), bf16),
            pltpu.VMEM((dsteps, N, ROWS, HD), bf16),
            pltpu.VMEM((KVH, ROWS, HD), f32),
            dma((NG,)), dma((NG,)), dma((ND,)),
            dma((HOLD,)), dma((HOLD,)),
            dma((N,)), dma((1,)),
            dma((1,)), dma((HOLD,)),
            dma((15,)), dma((N,)),
            dma((1,)), dma((HOLD,)),
            dma((dsteps // 2,)), dma((dsteps // 2,)),
        ],
        compiler_params=pltpu.CompilerParams(
            collective_id=0, has_side_effects=True, vmem_limit_bytes=60 * 1024 * 1024
        ),
    )(
        old_cache, new_slot.reshape(1, -1), lengths, old_angle.T, new_angle.T, queries,
        new_kv, resid, gain.reshape(1, -1), w_gate, w_up, w_down,
    )
    return new_cache, out


def rotate_block(block, where_pos, old_angle, new_angle):
    rows_here = block.shape[0]
    half_size = HD // 2
    parts = block.reshape(rows_here, 2, KVH, HD)
    keys = parts[:, 0].astype(jnp.float32)
    delta = jnp.take(new_angle, where_pos, axis=0) - jnp.take(old_angle, where_pos, axis=0)
    cosine = jnp.cos(delta)[:, None, :]
    sine = jnp.sin(delta)[:, None, :]
    first = keys[..., :half_size]
    second = keys[..., half_size:]
    turned = jnp.concatenate(
        [first * cosine - second * sine, second * cosine + first * sine], axis=-1
    ).astype(jnp.bfloat16)
    return jnp.stack([turned, parts[:, 1]], axis=1).reshape(rows_here, 2 * KVH * HD)


def per_device(
    old_cache,
    new_slot,
    lengths,
    old_angle,
    new_angle,
    queries,
    new_kv,
    resid,
    gain,
    w_gate,
    w_up,
    w_down,
):
    devices = lax.axis_size("ctx")
    own_index = lax.axis_index("ctx")
    slot_count = old_cache.shape[0]
    row_width = old_cache.shape[1]
    per_peer = slot_count // devices
    rows_dev = queries.shape[0]
    all_rows = rows_dev * devices
    group_size = QH // KVH
    high = lax.Precision.HIGHEST
    scale = 1.0 / float(HD) ** 0.5
    tokens = own_index * slot_count + jnp.arange(slot_count, dtype=jnp.int32)
    requests = jnp.arange(lengths.shape[0], dtype=jnp.int32)
    row_ends = jnp.sum(jnp.where(requests[None, :] <= requests[:, None], lengths[None, :], 0), axis=1)
    passed = row_ends[None, :] <= tokens[:, None]
    owner_row = jnp.minimum(jnp.sum(passed.astype(jnp.int32), axis=1), lengths.shape[0] - 1)
    row_prior = jnp.sum(jnp.where(passed, lengths[None, :], 0), axis=1)
    position = jnp.clip(tokens - row_prior, 0, old_angle.shape[0] - 1)
    filled = new_slot >= 0
    all_queries = lax.all_gather(queries, "ctx", axis=0, tiled=True)
    target = jnp.where(
        filled, new_slot // CTOK_DEV, jnp.arange(slot_count, dtype=jnp.int32) // per_peer
    )
    sorted_order = jnp.argsort(target, stable=True)
    new_place = jnp.where(filled, new_slot % CTOK_DEV, -1)
    slot_info = jnp.stack([new_place, owner_row, position], axis=1)[sorted_order]
    sent_rows = old_cache[sorted_order].reshape(devices, per_peer, row_width)
    got_rows = lax.all_to_all(sent_rows, "ctx", split_axis=0, concat_axis=0, tiled=True)
    got_info = lax.all_to_all(
        slot_info.reshape(devices, per_peer, 3), "ctx", split_axis=0, concat_axis=0, tiled=True
    )
    got_rows = got_rows.reshape(slot_count, row_width)
    got_info = got_info.reshape(slot_count, 3)
    landing = jnp.where(got_info[:, 0] >= 0, got_info[:, 0], CTOK_DEV)
    placed = jnp.zeros((CTOK_DEV, row_width), jnp.bfloat16).at[landing].set(got_rows, mode="drop")
    placed_row = jnp.zeros((CTOK_DEV,), jnp.int32).at[landing].set(got_info[:, 1], mode="drop")
    placed_pos = jnp.zeros((CTOK_DEV,), jnp.int32).at[landing].set(got_info[:, 2], mode="drop")
    placed, moved_row, moved_pos = (placed, placed_row, placed_pos)
    new_cache = rotate_block(placed, moved_pos, old_angle, new_angle)
    key_count = new_cache.shape[0]
    key_split = new_cache.reshape(key_count, 2, KVH, HD)
    value_four = key_split[:, 1].astype(jnp.float32)
    query_four = all_queries.reshape(all_rows, KVH, group_size, HD)
    scores = (
        jnp.einsum(
            "mjge,cje->mjgc", query_four, key_split[:, 0], preferred_element_type=jnp.float32
        )
        * scale
    )
    query_row = jnp.arange(all_rows, dtype=jnp.int32) // (2 * SAMPLES)
    matching = query_row[:, None] == moved_row[None, :]
    scores = jnp.where(matching[:, None, None, :], scores, -1e30)
    local_top = jnp.max(scores, axis=-1)
    own_query = queries.reshape(rows_dev, KVH, group_size, HD).astype(jnp.float32)
    fresh_kv = jnp.repeat(new_kv.reshape(rows_dev // 2, 2, 2, KVH, HD), 2, axis=0).astype(
        jnp.float32
    )
    own_steps = (
        jnp.arange(2, dtype=jnp.int32)[None, :]
        <= (jnp.arange(rows_dev, dtype=jnp.int32) % 2)[:, None]
    )
    own_scores = jnp.einsum("mjge,msje->mjgs", own_query, fresh_kv[:, :, 0], precision=high) * scale
    own_scores = jnp.where(own_steps[:, None, None, :], own_scores, -1e30)
    own_top = jnp.max(own_scores, axis=-1)
    floor_top = jnp.maximum(local_top, -10000.0)
    weights_local = jnp.exp(scores - floor_top[..., None])
    summed = jnp.einsum("mjgc,cje->mjge", weights_local, value_four, precision=high)
    totals = jnp.sum(weights_local, axis=-1)
    got_sums, got_totals, got_tops = (
        lax.all_to_all(
            summed.reshape(devices, rows_dev, QH * HD),
            "ctx",
            split_axis=0,
            concat_axis=0,
            tiled=True,
        ),
        lax.all_to_all(
            totals.reshape(devices, rows_dev, QH), "ctx", split_axis=0, concat_axis=0, tiled=True
        ),
        lax.all_to_all(
            floor_top.reshape(devices, rows_dev, QH), "ctx", split_axis=0, concat_axis=0, tiled=True
        ),
    )
    got_tops = got_tops.reshape(devices, rows_dev, KVH, group_size)
    row_top = jnp.maximum(jnp.max(got_tops, axis=0), own_top)
    rescale = jnp.exp(got_tops - row_top[None])
    weights_own = jnp.exp(own_scores - row_top[..., None])
    row_sums = jnp.sum(
        rescale[..., None] * got_sums.reshape(devices, rows_dev, KVH, group_size, HD), axis=0
    )
    row_sums = row_sums + jnp.einsum(
        "mjgs,msje->mjge", weights_own, fresh_kv[:, :, 1], precision=high
    )
    row_totals = jnp.sum(
        rescale * got_totals.reshape(devices, rows_dev, KVH, group_size), axis=0
    ) + jnp.sum(weights_own, axis=-1)
    attn = (row_sums / row_totals[..., None]).reshape(rows_dev, QH * HD)
    hstate = resid.astype(jnp.float32) + attn
    normed = (
        hstate
        * lax.rsqrt(jnp.mean(hstate * hstate, axis=-1, keepdims=True) + 1e-05)
        * gain.astype(jnp.float32)
    ).astype(jnp.bfloat16)
    piece = lax.all_gather(normed, "ctx", axis=0, tiled=True)
    gate_out = jnp.dot(piece, w_gate, preferred_element_type=jnp.float32)
    up_out = jnp.dot(piece, w_up, preferred_element_type=jnp.float32)
    hidden_all = (jax.nn.silu(gate_out) * up_out).astype(jnp.bfloat16)
    ffn_out = lax.psum_scatter(
        jnp.dot(hidden_all, w_down, preferred_element_type=jnp.float32),
        "ctx",
        scatter_dimension=0,
        tiled=True,
    )
    layer_out = (hstate + ffn_out).astype(jnp.bfloat16)
    return (new_cache, layer_out)


def solution(mesh):
    return jax.shard_map(
        fused if mesh.shape["ctx"] == N else per_device,
        mesh=mesh,
        in_specs=(
            P(("groups", "ctx"), None),
            P(("groups", "ctx")),
            P("groups"),
            P(),
            P(),
            P(("groups", "ctx"), None),
            P(("groups", "ctx"), None),
            P(("groups", "ctx"), None),
            P(),
            P(None, "ctx"),
            P(None, "ctx"),
            P("ctx", None),
        ),
        out_specs=(P(("groups", "ctx"), None), P(("groups", "ctx"), None)),
        check_vma=False,
    )
```
